256 devices in a mesh: chan: 64 (over z, x, y_lo), tm: 4 (over y_hi, core).
Axes of the slice: x: 4, y: 4 (y_hi: 2, y_lo: 2; y = y_hi * 2 + y_lo), z: 8, core: 2. Of those that a mesh axis runs over, the one named last changes fastest.
Arguments:
- traces: bfloat16 [128, 1024, 3000], P('tm', 'chan'), may hold values from -6 to 6
- valid: int32 [128, 1024], P('tm', 'chan'), may hold values 0 or 1
- sources: int32 [512], replicated, may hold values from 0 to 1023, as said below
Outputs:
- cross: bfloat16 [2, 1024, 512, 1024], P(None, ('chan', 'tm'))
The draws below stay inside these ranges and needn't reach their ends.
Inputs may be any that keep to these rules, and one draw needn't show every extreme that they name: `sources`: distinct channel indices; channels 0 and 1023 are always among them.
All inputs are finite; a program needn't handle non-finite values. No bound on the sum of `valid` on one device may be relied on, other than what follows from the above.
Results may differ from the reference program's by a relative error of at most 0.0066.
Values may be sent and summed in bfloat16 or wider, within the bound.
A program may use at most 128 MiB of HBM per device.

```python
import math
import jax
import jax.numpy as jnp
from jax import lax

NT = 3000
F = 1024
LOW_BIN = 6
HALF_SPAN = 32
CH = 1024
S = 512
WIN = 128


def draw_sources(key, part):
    key = jax.random.fold_in(key, 11)
    middle = 1 + jax.random.permutation(key, CH - 2)[:S - 2]
    picked = jnp.concatenate([jnp.array([0, CH - 1], dtype=jnp.int32), middle.astype(jnp.int32)])
    return jax.random.permutation(jax.random.fold_in(key, 1), picked).astype(jnp.int32)


def place_ends(drawn, stream_key, least, top_value):
    shape = drawn.shape
    index_at = [jax.random.randint(jax.random.fold_in(stream_key, axis), (), 0, shape[axis]) for axis in range(len(shape))]
    drawn = drawn.at[tuple(index_at)].set(least)
    longest = shape.index(max(shape))
    index_at[longest] = (index_at[longest] + 1) % shape[longest]
    return drawn.at[tuple(index_at)].set(top_value)


def block_levels(own_key, extent, shards, smallest, top_value):
    gain, own = 1.0, jax.random.fold_in(own_key, 6)
    for dim, shards_of in shards:
        heights = jnp.exp(jax.random.uniform(jax.random.fold_in(own, dim), (shards_of,), jnp.float32, smallest / len(shards), top_value / len(shards)))
        gain = gain * jnp.repeat(heights, extent[dim] // shards_of).reshape([-1 if axis == dim else 1 for axis in range(len(extent))])
    return gain


def gaussian(stream_key, shape, deviation, bound, cuts=(), kind=jnp.bfloat16):
    values = jax.random.normal(stream_key, shape, jnp.float32) * deviation
    if len(cuts) > 0:
        values = block_levels(stream_key, shape, cuts, -0.22, 0.18) * values
    return jnp.clip(values, min=-bound, max=bound).astype(kind)


def setup_inputs(seed: int = 0) -> dict:
    key_of = jax.random.split(jax.random.key(seed), 4)
    return {
        "traces": gaussian(key_of[0], (WIN, CH, NT), 1.0, 6.0, ((0, 4), (1, 64))),
        "valid": place_ends((jax.random.randint(key_of[1], (WIN, CH), 0, 8) < 7).astype(jnp.int32), jax.random.fold_in(key_of[1], 1), 0, 1),
        "sources": draw_sources(jax.random.fold_in(key_of[3], 71), 0),
    }


def dft_tables(first_bin, count, samples):
    times = jnp.arange(samples, dtype=jnp.int32)
    bins = LOW_BIN + first_bin + jnp.arange(count, dtype=jnp.int32)
    phase = times[:, None] * bins[None, :] % samples
    angle = 2.0 * math.pi / samples * phase.astype(jnp.float32)
    taper = 0.5 - 0.5 * jnp.cos(2.0 * math.pi / samples * times.astype(jnp.float32))
    cosine = (taper[:, None] * jnp.cos(angle)).astype(jnp.bfloat16)
    sine = (taper[:, None] * jnp.sin(angle)).astype(jnp.bfloat16)
    return (cosine, sine)

def band_ones(nbins):
    index = jnp.arange(nbins, dtype=jnp.int32)
    inside = (jnp.abs(index[:, None] - index[None, :]) <= HALF_SPAN).astype(jnp.float32)
    return (inside.astype(jnp.bfloat16), lax.optimization_barrier(jnp.sum(inside, axis=0)))

def reference(traces, valid, sources):
    windows, channels, samples = traces.shape
    sample_rows = traces.reshape(windows * channels, samples)
    block_size = min(F, 256)
    parts_re = []
    parts_im = []
    for first_bin in range(0, F, block_size):
        cosine, sine = dft_tables(first_bin, block_size, samples)
        parts_re.append(jnp.dot(sample_rows, cosine, preferred_element_type=jnp.float32))
        parts_im.append(-jnp.dot(sample_rows, sine, preferred_element_type=jnp.float32))
    real_part = jnp.concatenate(parts_re, axis=1)
    imag_part = jnp.concatenate(parts_im, axis=1)
    amplitude = jnp.sqrt(real_part * real_part + imag_part * imag_part).astype(jnp.bfloat16)
    ones_band, counts = band_ones(F)
    smooth = jnp.dot(amplitude, ones_band, preferred_element_type=jnp.float32) / counts[None, :]
    scale = valid.reshape(windows * channels, 1).astype(jnp.float32) / (smooth + 1e-06)
    white_re = (real_part * scale).astype(jnp.bfloat16).reshape(windows, channels, F)
    white_im = (imag_part * scale).astype(jnp.bfloat16).reshape(windows, channels, F)
    source_re = jnp.take(white_re, sources, axis=1)
    source_im = jnp.take(white_im, sources, axis=1)
    nblocks = F // 16

    def blocked(array):
        moved = jnp.transpose(array, (2, 0, 1))
        return moved.reshape(nblocks, 16, windows, array.shape[1])

    def one_block(pieces):
        s_re, s_im, c_re, c_im = [p.astype(jnp.float32) for p in pieces]
        cross_re = jnp.einsum('fws,fwc->fsc', s_re, c_re) + jnp.einsum('fws,fwc->fsc', s_im, c_im)
        cross_im = jnp.einsum('fws,fwc->fsc', s_re, c_im) - jnp.einsum('fws,fwc->fsc', s_im, c_re)
        return jnp.stack([cross_re, cross_im], axis=0).astype(jnp.bfloat16)
    stacked = lax.map(one_block, (blocked(source_re), blocked(source_im), blocked(white_re), blocked(white_im)))
    stacked = jnp.transpose(stacked, (1, 0, 2, 3, 4))
    return stacked.reshape(2, F, sources.shape[0], channels)
```

```python
import functools
import math

import jax
import jax.numpy as jnp
import numpy as np
from jax import lax
from jax.experimental import pallas as pl
from jax.experimental.pallas import tpu as pltpu
from jax.sharding import PartitionSpec as P

MESH = pl.DeviceIdType.MESH
F = 1024
LOW_BIN = 6
HALF_SPAN = 32
NT = 3000
NTP = 3072
DEVS = 256
PLANE = 32
BINS = 4
ROWS = 512
LANES = 256
CHUNKS = ROWS // LANES
Z_ORDER = (4, 0, 3, 5, 2, 6, 1, 7)
BF, F32 = jnp.bfloat16, jnp.float32


def tables():
    t = np.arange(NT, dtype=np.int64)
    k = LOW_BIN + np.arange(F, dtype=np.int64)
    angle = 2.0 * math.pi / NT * ((k[:, None] * t[None, :]) % NT)
    taper = 0.5 - 0.5 * np.cos(2.0 * math.pi / NT * t)
    re = (taper * np.cos(angle)).astype(np.float32)
    im = (-taper * np.sin(angle)).astype(np.float32)
    both = np.stack([re.reshape(DEVS, BINS, NT), im.reshape(DEVS, BINS, NT)], axis=1)
    out = np.zeros((2 * F, NTP), dtype=np.float32)
    out[:, :NT] = both.reshape(2 * F, NT)
    return out.astype(BF)


def me_at():
    ch, t = lax.axis_index("chan"), lax.axis_index("tm")
    return ch // 8, (ch // 2) % 4, (t // 2) * 2 + ch % 2, t % 2


def ids(z, x, y, c):
    return {"chan": z * 8 + x * 2 + y % 2, "tm": (y // 2) * 2 + c}


def linear(z, x, y, c):
    return (z * 8 + x * 2 + y % 2) * 4 + (y // 2) * 2 + c


def iota(shape, dim):
    return lax.broadcasted_iota(jnp.int32, shape, dim)


def front_kernel(x_hbm, t_hbm, valid_ref, d_hbm, xv, tv, xt, spec, amp, sendbuf, recv, perm, dbuf, x_sem, t_sem, send_sem, recv_sem, d_sem, sx, sy, sc):
    z, x, y, c = me_at()
    mine = linear(z, x, y, c)

    x_copies = [pltpu.make_async_copy(x_hbm.at[pl.ds(h * LANES, LANES)], xv.at[pl.ds(h * LANES, LANES)], x_sem.at[h]) for h in range(CHUNKS)]
    x_copies[0].start()

    def t_copy(b):
        rows = pl.ds(b * 256, 256)
        return pltpu.make_async_copy(t_hbm.at[rows], tv.at[rows], t_sem.at[b])

    for b in range(8):
        t_copy(b).start()
        if b == 0:
            x_copies[1].start()

    line_z = [((z + i) % 8, x, y, c) for i in range(1, 8)]
    line_x = [(z, (x + i) % 4, y, c) for i in range(1, 4)]
    line_y = [(z, x, (y + i) % 4, c) for i in range(1, 4)]
    line_c = [(z, x, y, 1 - c)]
    barrier = pltpu.get_barrier_semaphore()
    for q in line_z + line_x + line_y + line_c:
        pl.semaphore_signal(barrier, inc=1, device_id=ids(*q), device_id_type=MESH)

    def signal(line, sem):
        for q in line:
            pl.semaphore_signal(sem, inc=1, device_id=ids(*q), device_id_type=MESH)

    spread = (iota((16, LANES), 1) % 16 == iota((16, LANES), 0)).astype(F32)
    by_channel = jnp.dot(valid_ref[...].astype(F32), spread, preferred_element_type=F32)
    low = iota((1, 8, LANES), 1) < 4
    band = (jnp.abs(iota((128, 256), 0) + 64 - iota((128, 256), 1)) <= HALF_SPAN).astype(BF)
    amp[0:64, :] = jnp.zeros((64, LANES), BF)
    amp[64 + F:, :] = jnp.zeros((64, LANES), BF)
    xt[NTP - 128:, :] = jnp.zeros((128, ROWS), BF)

    def transform(h, first):
        lanes = slice(h * LANES, (h + 1) * LANES)
        x_copies[h].wait()
        for j in range(NT // 128):
            cols = slice(j * 128, (j + 1) * 128)
            xt[cols, lanes] = xv[lanes, cols].T
        tail = NT // 128 * 128
        xt[tail:NT, lanes] = xv[lanes, tail:NT].T

        def block(b, carry):
            if first:
                t_copy(b).wait()
            rows = pl.ds(pl.multiple_of(b * 256, 256), 256)
            out = jnp.dot(tv[rows, :], xt[:, lanes], preferred_element_type=F32)
            spec[rows, :] = out
            sq = (out * out).reshape(16, 2, 8, LANES)
            a, bb = sq[:, 0], sq[:, 1]
            total = jnp.where(low, a, bb) + pltpu.roll(jnp.where(low, bb, a), 4, 1)
            at = pl.ds(pl.multiple_of(64 + b * 128, 64), 128)
            amp[at, :] = jnp.sqrt(total).reshape(128, LANES).astype(BF)
            return carry

        lax.fori_loop(0, 8, block, 0)
        mask = iota((32, LANES), 0) == h * (LANES // 16) + iota((32, LANES), 1) // 16
        valid = jnp.sum(jnp.where(mask, by_channel, 0.0), axis=0, keepdims=True)

        def whiten(b, carry):
            total = jnp.dot(band, amp[pl.ds(pl.multiple_of(b * 128, 128), 256), :], preferred_element_type=F32)
            k = b * 128 + iota((128, LANES), 0)
            count = jnp.minimum(k + HALF_SPAN, F - 1) - jnp.maximum(k - HALF_SPAN, 0) + 1
            scale = (valid / (total / count.astype(F32) + 1e-6)).reshape(16, 8, LANES)
            turned = pltpu.roll(scale, 4, 1)
            s = spec[pl.ds(pl.multiple_of(b * 256, 256), 256), :].reshape(16, 2, 8, LANES)
            wa = s[:, 0] * jnp.where(low, scale, turned)
            wb = s[:, 1] * jnp.where(low, turned, scale)
            w = jnp.stack([wa, wb], axis=1)
            w = jnp.concatenate([w[..., :128], w[..., 128:]], axis=2)
            sendbuf[h, pl.ds(b * 32, 32)] = w.reshape(32, 16, 128).astype(BF)
            return carry

        lax.fori_loop(0, 8, whiten, 0)

    def send(h):
        own = pltpu.make_async_copy(sendbuf.at[h, mine], recv.at[h, mine], recv_sem.at[h, 0])
        own.start()
        for g in range(0, 8, 2):
            pair = Z_ORDER[g:g + 2]

            def one(n, carry):
                for off in pair:
                    q = ((z + off) % 8, (x + n // 8) % 4, (y + n // 2) % 4, (c + n) % 2)

                    def go():
                        pltpu.make_async_remote_copy(
                            src_ref=sendbuf.at[h, linear(*q)], dst_ref=recv.at[h, mine], send_sem=send_sem.at[h],
                            recv_sem=recv_sem.at[h, off], device_id=ids(*q), device_id_type=MESH).start()

                    if off == 0:
                        pl.when(n > 0)(go)
                    else:
                        go()
                return carry

            lax.fori_loop(0, PLANE, one, 0)

    transform(0, True)
    pl.semaphore_wait(barrier, 14)
    for line, sem in ((line_x, sx), (line_y, sy), (line_c, sc)):
        signal(line, sem)
        pl.semaphore_wait(sem, len(line))
    send(0)
    transform(1, False)
    send(1)

    frm, to = iota((1024, 1024), 0), iota((1024, 1024), 1)
    perm[...] = (to == (frm // 16 % 8) * 128 + (frm // 128) * 16 + frm % 16).astype(BF)
    r, p = iota((128, 128), 1), iota((128, 128), 0)
    row_perm = (p == (r % 4) * 32 + (r // 4 % 2) * 16 + r // 8).astype(BF)

    out_copies = []
    for g in range(8):
        off = Z_ORDER[g]
        zs = (z + 8 - off) % 8
        part = pl.ds(zs * PLANE, PLANE)
        for h in range(CHUNKS):
            pltpu.make_async_copy(sendbuf.at[h, pl.ds(0, PLANE)], recv.at[h, part], recv_sem.at[h, off]).wait()
        got = recv[:, part].reshape(CHUNKS, 8, 4, 16, 128)
        wide = jnp.concatenate([got[:, i].reshape(128, 128) for i in range(8)], axis=1)
        g1 = jnp.dot(row_perm, wide, preferred_element_type=F32).astype(BF)
        g2 = jnp.dot(g1, perm[...], preferred_element_type=F32).astype(BF)
        for f in range(BINS):
            for ri in range(2):
                for w in range(8):
                    dbuf[g, f, ri * 128 + w * 16:ri * 128 + w * 16 + 16, :] = g2[(f * 2 + ri) * 16:(f * 2 + ri) * 16 + 16, w * 128:w * 128 + 128]
        out = pltpu.make_async_copy(dbuf.at[g], d_hbm.at[:, zs], d_sem.at[g])
        out.start()
        out_copies.append(out)
    for out in out_copies:
        out.wait()
    for h in range(CHUNKS):
        pltpu.make_async_copy(sendbuf.at[h, pl.ds(0, DEVS - 1)], recv.at[h, pl.ds(0, DEVS - 1)], send_sem.at[h]).wait()


def cross_kernel(src_ref, d_ref, o_ref, pick, chosen):
    f, ri = pl.program_id(0), pl.program_id(1)

    @pl.when((f == 0) & (ri == 0))
    def _():
        pick[...] = (iota((1024, 512), 0) == src_ref[...]).astype(BF)

    def chans():
        return jnp.concatenate([d_ref[0, i] for i in range(8)], axis=1)

    @pl.when(ri == 0)
    def _():
        cc = chans()
        s = jnp.dot(cc, pick[...], preferred_element_type=F32).astype(BF)
        chosen[...] = s.T
        o_ref[0, 0] = jnp.dot(chosen[...], cc, preferred_element_type=F32).astype(BF)

    @pl.when(ri == 1)
    def _():
        cc = chans()
        cc = jnp.concatenate([cc[128:], -cc[:128]], axis=0)
        o_ref[0, 0] = jnp.dot(chosen[...], cc, preferred_element_type=F32).astype(BF)


def body(table, traces, valid, sources):
    rows = traces.reshape(ROWS, NT)
    any_spec = pl.BlockSpec(memory_space=pl.ANY)
    vmem = pl.BlockSpec(memory_space=pltpu.VMEM)
    d = pl.pallas_call(
        front_kernel,
        out_shape=jax.ShapeDtypeStruct((BINS, 8, 256, 128), BF),
        in_specs=[any_spec, any_spec, vmem],
        out_specs=any_spec,
        scratch_shapes=[
            pltpu.VMEM((ROWS, NT), BF),
            pltpu.VMEM((2 * F, NTP), BF),
            pltpu.VMEM((NTP, ROWS), BF),
            pltpu.VMEM((2 * F, LANES), F32),
            pltpu.VMEM((F + 128, LANES), BF),
            pltpu.VMEM((CHUNKS, DEVS, 16, 128), BF),
            pltpu.VMEM((CHUNKS, DEVS, 16, 128), BF),
            pltpu.VMEM((1024, 1024), BF),
            pltpu.VMEM((8, BINS, 256, 128), BF),
            pltpu.SemaphoreType.DMA((CHUNKS,)),
            pltpu.SemaphoreType.DMA((8,)),
            pltpu.SemaphoreType.DMA((CHUNKS,)),
            pltpu.SemaphoreType.DMA((CHUNKS, 8)),
            pltpu.SemaphoreType.DMA((8,)),
            pltpu.SemaphoreType.REGULAR,
            pltpu.SemaphoreType.REGULAR,
            pltpu.SemaphoreType.REGULAR,
        ],
        compiler_params=pltpu.CompilerParams(collective_id=0, has_side_effects=True, vmem_limit_bytes=56 * 2**20),
    )(rows, table, valid)
    return pl.pallas_call(
        cross_kernel,
        grid=(BINS, 2),
        out_shape=jax.ShapeDtypeStruct((2, BINS, 512, 1024), BF),
        in_specs=[pl.BlockSpec((1, 512), lambda f, r: (0, 0)), pl.BlockSpec((1, 8, 256, 128), lambda f, r: (f, 0, 0, 0))],
        out_specs=pl.BlockSpec((1, 1, 512, 1024), lambda f, r: (r, f, 0, 0)),
        scratch_shapes=[pltpu.VMEM((1024, 512), BF), pltpu.VMEM((512, 256), BF)],
        compiler_params=pltpu.CompilerParams(vmem_limit_bytes=48 * 2**20),
    )(sources.reshape(1, 512), d)


def solution(mesh):
    table = tables()

    def whole(traces, valid, sources):
        placed = (P(), P("tm", "chan", None), P("tm", "chan"), P())
        return jax.shard_map(
            body,
            mesh=mesh,
            in_specs=placed,
            out_specs=P(None, ("chan", "tm"), None, None),
            check_vma=False,
        )(jnp.asarray(table), traces, valid, sources)

    return whole
```

```python
import functools
import math

import jax
import jax.numpy as jnp
import numpy as np
from jax import lax
from jax.experimental import pallas as pl
from jax.experimental.pallas import tpu as pltpu
from jax.sharding import PartitionSpec as P

MESH = pl.DeviceIdType.MESH
F = 1024
LOW_BIN = 6
HALF_SPAN = 32
NT = 3000
NTP = 3072
HALF = NTP // 2
DEVS = 256
PLANE = 32
BINS = 4
ROWS = 512
LANES = 256
CHUNKS = ROWS // LANES
PHASES = ((4, 1), (3, 7), (5, 0), (2, 6))
ARRIVAL = (4, 1, 7, 3, 5, 0, 2, 6)
BF, F32 = jnp.bfloat16, jnp.float32


def tables():
    t = np.arange(HALF, dtype=np.int64)
    k = LOW_BIN + np.arange(F, dtype=np.int64)
    angle = 2.0 * math.pi / NT * ((k[:, None] * t[None, :]) % NT)
    taper = 0.5 - 0.5 * np.cos(2.0 * math.pi / NT * t)
    weight = np.where(t < NT // 2, 1.0, np.where(t == NT // 2, 0.5, 0.0)) * taper
    return np.stack([weight * np.cos(angle), -weight * np.sin(angle)]).astype(np.float32).astype(BF)


def me_at():
    ch, t = lax.axis_index("chan"), lax.axis_index("tm")
    return ch // 8, (ch // 2) % 4, (t // 2) * 2 + ch % 2, t % 2


def ids(z, x, y, c):
    return {"chan": z * 8 + x * 2 + y % 2, "tm": (y // 2) * 2 + c}


def linear(z, x, y, c):
    return (z * 8 + x * 2 + y % 2) * 4 + (y // 2) * 2 + c


def iota(shape, dim):
    return lax.broadcasted_iota(jnp.int32, shape, dim)


def front_kernel(x_hbm, t_hbm, valid_ref, src_ref, d_hbm, s_hbm, xv, tv, xt, plus, minus, spec, amp, inv, sendbuf, recv, perm, pick, dbuf, chosen, x_sem, t_sem, send_sem, recv_sem, d_sem, s_sem, here):
    z, x, y, c = me_at()
    mine = linear(z, x, y, c)
    sign = 1 - 2 * c

    def plane_at(i):
        return lax.rem(z + 12 + sign * i, 8)

    x_copies = [pltpu.make_async_copy(x_hbm.at[pl.ds(h * LANES, LANES)], xv.at[pl.ds(h * LANES, LANES)], x_sem.at[h]) for h in range(CHUNKS)]
    x_copies[0].start()

    def t_copy(i):
        rows = pl.ds(pl.multiple_of(plane_at(i - 1) * 128, 128), 128)
        return pltpu.make_async_copy(t_hbm.at[:, rows], tv.at[:, rows], t_sem.at[i])

    for i in range(8):
        t_copy(i).start()
    x_copies[1].start()

    column = [((z + i) % 8, x, y, (c + j) % 2) for i in range(8) for j in range(2) if i or j]
    plane = [(z, (x + i) % 4, (y + j) % 4, c) for i in range(4) for j in range(4) if i or j]
    barrier = pltpu.get_barrier_semaphore()
    for q in column + plane:
        pl.semaphore_signal(barrier, inc=1, device_id=ids(*q), device_id_type=MESH)

    spread = (iota((16, LANES), 1) % 16 == iota((16, LANES), 0)).astype(F32)
    by_channel = lax.dot_general(valid_ref[...].astype(F32), spread, (((0,), (0,)), ((), ())), preferred_element_type=F32)
    low = iota((1, 8, LANES), 1) < 4
    band = (jnp.abs(iota((128, 256), 0) + 64 - iota((128, 256), 1)) <= HALF_SPAN).astype(BF)
    back = (iota((128, 256), 0) + iota((128, 256), 1) == NT - 22 * 128).astype(BF)
    k = iota((F, LANES), 0)
    inv[...] = 1.0 / (jnp.minimum(k + HALF_SPAN, F - 1) - jnp.maximum(k - HALF_SPAN, 0) + 1).astype(F32)
    amp[0:64, :] = jnp.zeros((64, LANES), BF)
    amp[64 + F:, :] = jnp.zeros((64, LANES), BF)
    xt[NTP - 128:, :] = jnp.zeros((128, ROWS), BF)

    def fold(h):
        lanes = slice(h * LANES, (h + 1) * LANES)
        x_copies[h].wait()
        for j in range(NT // 128):
            cols = slice(j * 128, (j + 1) * 128)
            xt[cols, lanes] = xv[lanes, cols].T
        tail = NT // 128 * 128
        xt[tail:NT, lanes] = xv[lanes, tail:NT].T
        for m in range(HALF // 128):
            at, there = slice(m * 128, m * 128 + 128), (22 - m) * 128
            ahead = xt[at, lanes].astype(F32)
            behind = jnp.dot(back, xt[there:there + 256, lanes], preferred_element_type=F32)
            for total, out in ((ahead + behind, plus), (ahead - behind, minus)):
                rounded = total.astype(BF)
                out[at, :LANES] = rounded
                out[at, LANES:] = (total - rounded.astype(F32)).astype(BF)

    def block(first, n):
        rows = pl.ds(first, n)
        re = jnp.dot(tv[0, rows, :], plus[...], preferred_element_type=F32)
        im = jnp.dot(tv[1, rows, :], minus[...], preferred_element_type=F32)
        re = re[:, :LANES] + re[:, LANES:]
        im = im[:, :LANES] + im[:, LANES:]
        spec[0, rows, :] = re
        spec[1, rows, :] = im
        power = re * re + im * im
        amp[pl.ds(pl.multiple_of(64 + first, 64), n), :] = (power * lax.rsqrt(jnp.maximum(power, 1e-37))).astype(BF)

    def valid_row(h):
        mask = iota((32, LANES), 0) == h * (LANES // 16) + iota((32, LANES), 1) // 16
        return jnp.sum(jnp.where(mask, by_channel, 0.0), axis=0, keepdims=True)

    def whiten(h, b, valid):
        rows = pl.ds(pl.multiple_of(b * 128, 128), 128)
        total = jnp.dot(band, amp[pl.ds(pl.multiple_of(b * 128, 128), 256), :], preferred_element_type=F32)
        scale = valid / (total * inv[rows, :] + 1e-6)
        wr = (spec[0, rows, :] * scale).reshape(16, 8, LANES)
        wi = (spec[1, rows, :] * scale).reshape(16, 8, LANES)
        wa = jnp.where(low, wr, pltpu.roll(wi, 4, 1))
        wb = jnp.where(low, pltpu.roll(wr, 4, 1), wi)
        w = jnp.stack([wa, wb], axis=1)
        w = jnp.concatenate([w[..., :128], w[..., 128:]], axis=2)
        sendbuf[h, pl.ds(b * 32, 32)] = w.reshape(32, 16, 128).astype(BF)

    xs = [lax.rem(x + i, 4) for i in range(4)]
    ys = [lax.rem(y + i, 4) for i in range(4)]
    cs = [c, 1 - c]
    spots = [(xs[i] * 2 + lax.rem(ys[j], 2), lax.div(ys[j], 2) * 2 + cs[n]) for i in range(4) for j in range(4) for n in range(2)]

    def send(h, n, to, group):
        chan, tm = spots[n]
        chan = to * 8 + chan
        pltpu.make_async_remote_copy(
            src_ref=sendbuf.at[h, chan * 4 + tm], dst_ref=recv.at[h, mine], send_sem=send_sem.at[h],
            recv_sem=recv_sem.at[h, group], device_id={"chan": chan, "tm": tm}, device_id_type=MESH).start()

    fold(0)
    pl.semaphore_wait(barrier, 30)
    for q in plane:
        pl.semaphore_signal(here, inc=1, device_id=ids(*q), device_id_type=MESH)
    valid = valid_row(0)

    def step(i, carry):
        @pl.when(i < 8)
        def _():
            t_copy(i).wait()
            block(pl.multiple_of(plane_at(i - 1) * 128, 128), 128)

        @pl.when(i >= 2)
        def _():
            to = plane_at(i - 2)
            whiten(0, to, valid)

            @pl.when(i == 2)
            def _():
                pl.semaphore_wait(here, 15)

            group = lax.rem(to + 8 - z, 8)

            @pl.when(group > 0)
            def _():
                send(0, 0, to, group)

            for n in range(1, PLANE):
                send(0, n, to, group)

        return carry

    lax.fori_loop(0, 10, step, 0)
    pltpu.make_async_copy(sendbuf.at[0, mine], recv.at[0, mine], recv_sem.at[0, 0]).start()

    fold(1)

    def wide_block(b, carry):
        block(pl.multiple_of(b * 256, 256), 256)
        return carry

    lax.fori_loop(0, 4, wide_block, 0)
    valid = valid_row(1)

    def whiten_1(b, carry):
        whiten(1, b, valid)
        return carry

    lax.fori_loop(0, 8, whiten_1, 0)
    pltpu.make_async_copy(sendbuf.at[1, mine], recv.at[1, mine], recv_sem.at[1, 0]).start()
    for pair in PHASES:
        groups = [lax.rem(8 + sign * off, 8) for off in pair]
        planes = [lax.rem(z + g, 8) for g in groups]
        for n in range(PLANE):
            for off, g, to in zip(pair, groups, planes):
                if off or n:
                    send(1, n, to, g)

    frm, to = iota((1024, 1024), 0), iota((1024, 1024), 1)
    perm[...] = (to == (frm // 16 % 8) * 128 + (frm // 128) * 16 + frm % 16).astype(BF)
    r, p = iota((128, 128), 1), iota((128, 128), 0)
    row_perm = (p == (r % 4) * 32 + (r // 4 % 2) * 16 + r // 8).astype(BF)
    for i in range(8):
        pick[i] = (iota((128, 512), 0) + i * 128 == src_ref[...]).astype(BF).T

    out_copies = []
    for g in range(8):
        off = ARRIVAL[g]
        zs = lax.rem(z + 8 - off, 8)
        part = pl.ds(zs * PLANE, PLANE)
        for h in range(CHUNKS):
            pltpu.make_async_copy(sendbuf.at[h, pl.ds(0, PLANE)], recv.at[h, part], recv_sem.at[h, off]).wait()
        got = recv[:, part].reshape(CHUNKS, 8, 4, 16, 128)
        wide = jnp.concatenate([got[:, i].reshape(128, 128) for i in range(8)], axis=1)
        g1 = jnp.dot(row_perm, wide, preferred_element_type=F32).astype(BF)
        g2 = jnp.dot(g1, perm[...], preferred_element_type=F32).astype(BF)
        for f in range(BINS):
            bin_rows = []
            for ri in range(2):
                rows = slice((f * 2 + ri) * 16, (f * 2 + ri) * 16 + 16)
                bin_rows += [g2[rows, w * 128:w * 128 + 128] for w in range(8)]
            mat = jnp.concatenate(bin_rows, axis=0)
            dbuf[g, f] = mat
            chan_part = lax.dot_general(pick[zs], mat, (((1,), (1,)), ((), ())), preferred_element_type=F32).astype(BF)
            chosen[f] = chan_part if g == 0 else chosen[f] + chan_part
        out = pltpu.make_async_copy(dbuf.at[g], d_hbm.at[:, zs], d_sem.at[g])
        out.start()
        out_copies.append(out)
    out = pltpu.make_async_copy(chosen, s_hbm, s_sem)
    out.start()
    for out in out_copies + [out]:
        out.wait()
    for h in range(CHUNKS):
        pltpu.make_async_copy(sendbuf.at[h, pl.ds(0, DEVS - 1)], recv.at[h, pl.ds(0, DEVS - 1)], send_sem.at[h]).wait()


def cross_kernel(d_hbm, s_hbm, o_hbm, dv, chosen, buf, d_sem, s_sem, o_sem):
    copies = []
    for f in range(BINS):
        copies.append((pltpu.make_async_copy(d_hbm.at[f], dv.at[f], d_sem.at[f]), pltpu.make_async_copy(s_hbm.at[f], chosen.at[f], s_sem.at[f])))
        for copy in copies[-1]:
            copy.start()
    outs = []
    for f in range(BINS):
        for copy in copies[f]:
            copy.wait()
        cc = jnp.concatenate([dv[f, i] for i in range(8)], axis=1)
        for ri in range(2):
            if ri == 1:
                cc = jnp.concatenate([cc[128:], -cc[:128]], axis=0)
            for m in range(0, 512, 256):
                part = pl.ds(m, 256)
                buf[ri, f, part] = jnp.dot(chosen[f, part, :], cc, preferred_element_type=F32).astype(BF)
                out = pltpu.make_async_copy(buf.at[ri, f, part], o_hbm.at[ri, f, part], o_sem.at[ri, f, m // 256])
                out.start()
                outs.append(out)
    for out in outs:
        out.wait()


def body(table, traces, valid, sources):
    rows = traces.reshape(ROWS, NT)
    any_spec = pl.BlockSpec(memory_space=pl.ANY)
    vmem = pl.BlockSpec(memory_space=pltpu.VMEM)
    d, s = pl.pallas_call(
        front_kernel,
        out_shape=(jax.ShapeDtypeStruct((BINS, 8, 256, 128), BF), jax.ShapeDtypeStruct((BINS, 512, 256), BF)),
        in_specs=[any_spec, any_spec, vmem, vmem],
        out_specs=(any_spec, any_spec),
        scratch_shapes=[
            pltpu.VMEM((ROWS, NT), BF),
            pltpu.VMEM((2, F, HALF), BF),
            pltpu.VMEM((NTP, ROWS), BF),
            pltpu.VMEM((HALF, 2 * LANES), BF),
            pltpu.VMEM((HALF, 2 * LANES), BF),
            pltpu.VMEM((2, F, LANES), F32),
            pltpu.VMEM((F + 128, LANES), BF),
            pltpu.VMEM((F, LANES), F32),
            pltpu.VMEM((CHUNKS, DEVS, 16, 128), BF),
            pltpu.VMEM((CHUNKS, DEVS, 16, 128), BF),
            pltpu.VMEM((1024, 1024), BF),
            pltpu.VMEM((8, 512, 128), BF),
            pltpu.VMEM((8, BINS, 256, 128), BF),
            pltpu.VMEM((BINS, 512, 256), BF),
            pltpu.SemaphoreType.DMA((CHUNKS,)),
            pltpu.SemaphoreType.DMA((8,)),
            pltpu.SemaphoreType.DMA((CHUNKS,)),
            pltpu.SemaphoreType.DMA((CHUNKS, 8)),
            pltpu.SemaphoreType.DMA((8,)),
            pltpu.SemaphoreType.DMA,
            pltpu.SemaphoreType.REGULAR,
        ],
        compiler_params=pltpu.CompilerParams(collective_id=0, has_side_effects=True, vmem_limit_bytes=58 * 2**20),
    )(rows, table, valid.T, sources.reshape(1, 512))
    return pl.pallas_call(
        cross_kernel,
        out_shape=jax.ShapeDtypeStruct((2, BINS, 512, 1024), BF),
        in_specs=[any_spec, any_spec],
        out_specs=any_spec,
        scratch_shapes=[
            pltpu.VMEM((BINS, 8, 256, 128), BF),
            pltpu.VMEM((BINS, 512, 256), BF),
            pltpu.VMEM((2, BINS, 512, 1024), BF),
            pltpu.SemaphoreType.DMA((BINS,)),
            pltpu.SemaphoreType.DMA((BINS,)),
            pltpu.SemaphoreType.DMA((2, BINS, 2)),
        ],
        compiler_params=pltpu.CompilerParams(vmem_limit_bytes=60 * 2**20),
    )(d, s)


def solution(mesh):
    table = tables()

    def whole(traces, valid, sources):
        placed = (P(), P("tm", "chan", None), P("tm", "chan"), P())
        return jax.shard_map(
            body,
            mesh=mesh,
            in_specs=placed,
            out_specs=P(None, ("chan", "tm"), None, None),
            check_vma=False,
        )(jnp.asarray(table), traces, valid, sources)

    return whole
```

```python
import functools
import math

import jax
import jax.numpy as jnp
import numpy as np
from jax import lax
from jax.experimental import pallas as pl
from jax.experimental.pallas import tpu as pltpu
from jax.sharding import PartitionSpec as P

MESH = pl.DeviceIdType.MESH
F = 1024
LOW_BIN = 6
HALF_SPAN = 32
NT = 3000
NTP = 3072
HALF = NTP // 2
EDGE = 64
FAR = 4
DEVS = 256
PLANE = 32
BINS = 4
ROWS = 512
LANES = 256
CHUNKS = ROWS // LANES
PHASES = ((4, 1), (3, 7), (5, 0), (2, 6))
ARRIVAL = ((4,), (1, 7), (3, 5), (0,), (2, 6))
BF, F32 = jnp.bfloat16, jnp.float32


def tables():
    t = np.arange(HALF, dtype=np.int64)
    k = LOW_BIN + np.arange(F, dtype=np.int64)
    angle = 2.0 * math.pi / NT * ((k[:, None] * t[None, :]) % NT)
    taper = 0.5 - 0.5 * np.cos(2.0 * math.pi / NT * t)
    weight = np.where(t < NT // 2, 1.0, np.where(t == NT // 2, 0.5, 0.0)) * taper
    both = np.stack([weight * np.cos(angle), -weight * np.sin(angle)]).astype(np.float32)
    return np.pad(both, ((0, 0), (EDGE, EDGE), (0, 0))).astype(BF)


def me_at():
    ch, t = lax.axis_index("chan"), lax.axis_index("tm")
    return ch // 8, (ch // 2) % 4, (t // 2) * 2 + ch % 2, t % 2


def ids(z, x, y, c):
    return {"chan": z * 8 + x * 2 + y % 2, "tm": (y // 2) * 2 + c}


def linear(z, x, y, c):
    return (z * 8 + x * 2 + y % 2) * 4 + (y // 2) * 2 + c


def iota(shape, dim):
    return lax.broadcasted_iota(jnp.int32, shape, dim)


def front_kernel(x_hbm, t_hbm, small_ref, d_ref, s_ref, xv, tv, tv_first, xt, plus, minus, spec, amp, inv, sendbuf, recv, pick, x_sem, t_sem, send_sem, recv_sem, here):
    z, x, y, c = me_at()
    mine = linear(z, x, y, c)
    sign = 1 - 2 * c
    far = lax.rem(z + FAR, 8)

    x_copies = [pltpu.make_async_copy(x_hbm.at[pl.ds(h * LANES, LANES)], xv.at[pl.ds(h * LANES, LANES)], x_sem.at[h]) for h in range(CHUNKS)]
    first_rows = pl.ds(pl.multiple_of(far * 128 + EDGE - HALF_SPAN, 32), 128 + 2 * HALF_SPAN)
    first_copy = pltpu.make_async_copy(t_hbm.at[:, first_rows], tv_first, t_sem.at[4])

    def t_copy(b):
        rows = pl.ds(EDGE + b * 256, 256)
        return pltpu.make_async_copy(t_hbm.at[:, rows], tv.at[:, rows], t_sem.at[b])

    x_copies[0].start()
    first_copy.start()

    column = [((z + i) % 8, x, y, (c + j) % 2) for i in range(8) for j in range(2) if i or j]
    plane = [(z, (x + i) % 4, (y + j) % 4, c) for i in range(4) for j in range(4) if i or j]
    barrier = pltpu.get_barrier_semaphore()
    for q in column + plane:
        pl.semaphore_signal(barrier, inc=1, device_id=ids(*q), device_id_type=MESH)

    spread = (iota((16, LANES), 1) % 16 == iota((16, LANES), 0)).astype(F32)
    by_channel = lax.dot_general(small_ref[0:16, 0:32].astype(F32), spread, (((0,), (0,)), ((), ())), preferred_element_type=F32)
    low = iota((1, 8, LANES), 1) < 4
    band = (jnp.abs(iota((128, 256), 0) + 64 - iota((128, 256), 1)) <= HALF_SPAN).astype(BF)
    back = (iota((128, 256), 0) + iota((128, 256), 1) == NT - 22 * 128).astype(BF)
    k = iota((F, LANES), 0)
    inv[...] = 1.0 / (jnp.minimum(k + HALF_SPAN, F - 1) - jnp.maximum(k - HALF_SPAN, 0) + 1).astype(F32)
    amp[:EDGE, :] = jnp.zeros((EDGE, LANES), BF)
    amp[EDGE + F:, :] = jnp.zeros((EDGE, LANES), BF)
    xt[NTP - 128:, :] = jnp.zeros((128, ROWS), BF)

    def fold(h):
        lanes = slice(h * LANES, (h + 1) * LANES)
        x_copies[h].wait()
        for j in range(NT // 128):
            cols = slice(j * 128, (j + 1) * 128)
            xt[cols, lanes] = xv[lanes, cols].T
        tail = NT // 128 * 128
        xt[tail:NT, lanes] = xv[lanes, tail:NT].T
        for m in range(HALF // 128):
            at, there = slice(m * 128, m * 128 + 128), (22 - m) * 128
            ahead = xt[at, lanes].astype(F32)
            behind = jnp.dot(back, xt[there:there + 256, lanes], preferred_element_type=F32)
            for total, out in ((ahead + behind, plus), (ahead - behind, minus)):
                rounded = total.astype(BF)
                out[at, :LANES] = rounded
                out[at, LANES:] = (total - rounded.astype(F32)).astype(BF)

    def block(table, first, n):
        rows = pl.ds(first, n)
        re = jnp.dot(table[0], plus[...], preferred_element_type=F32)
        im = jnp.dot(table[1], minus[...], preferred_element_type=F32)
        re = re[:, :LANES] + re[:, LANES:]
        im = im[:, :LANES] + im[:, LANES:]
        spec[0, rows, :] = re
        spec[1, rows, :] = im
        power = re * re + im * im
        amp[rows, :] = (power * lax.rsqrt(jnp.maximum(power, 1e-37))).astype(BF)

    def valid_row(h):
        mask = iota((32, LANES), 0) == h * (LANES // 16) + iota((32, LANES), 1) // 16
        return jnp.sum(jnp.where(mask, by_channel, 0.0), axis=0, keepdims=True)

    def whiten(h, b, valid):
        at = pl.multiple_of(b * 128, 128)
        rows = pl.ds(pl.multiple_of(EDGE + at, EDGE), 128)
        total = jnp.dot(band, amp[pl.ds(at, 256), :], preferred_element_type=F32)
        scale = valid / (total * inv[pl.ds(at, 128), :] + 1e-6)
        wr = (spec[0, rows, :] * scale).reshape(16, 8, LANES)
        wi = (spec[1, rows, :] * scale).reshape(16, 8, LANES)
        wa = jnp.where(low, wr, pltpu.roll(wi, 4, 1))
        wb = jnp.where(low, pltpu.roll(wr, 4, 1), wi)
        w = jnp.stack([wa, wb], axis=1)
        w = jnp.concatenate([w[..., :128], w[..., 128:]], axis=2)
        sendbuf[h, pl.ds(b * 32, 32)] = w.reshape(32, 16, 128).astype(BF)

    def send(h, n, off):
        xn, yn = lax.rem(x + lax.div(n, 8), 4), lax.rem(y + lax.rem(lax.div(n, 2), 4), 4)
        chan = lax.rem(z + off, 8) * 8 + xn * 2 + lax.rem(yn, 2)
        tm = lax.div(yn, 2) * 2 + lax.rem(c + n, 2)
        pltpu.make_async_remote_copy(
            src_ref=sendbuf.at[h, chan * 4 + tm], dst_ref=recv.at[h, mine], send_sem=send_sem.at[h],
            recv_sem=recv_sem.at[h, off], device_id={"chan": chan, "tm": tm}, device_id_type=MESH).start()

    def send_planes(h, offs):
        def one(n, carry):
            for off in offs:
                if isinstance(off, int) and off == 0:
                    pl.when(n > 0)(functools.partial(send, h, n, 0))
                else:
                    send(h, n, off)
            return carry

        lax.fori_loop(0, PLANE, one, 0)
        if any(isinstance(off, int) and off == 0 for off in offs):
            pltpu.make_async_copy(sendbuf.at[h, mine], recv.at[h, mine], recv_sem.at[h, 0]).start()

    def relay():
        pl.semaphore_wait(barrier, 30)
        for q in plane:
            pl.semaphore_signal(here, inc=1, device_id=ids(*q), device_id_type=MESH)

    pl.when(z >= 4)(relay)
    fold(0)
    for b in range(4):
        t_copy(b).start()
    x_copies[1].start()
    valid = valid_row(0)
    first_copy.wait()
    block(tv_first, pl.multiple_of(far * 128 + EDGE - HALF_SPAN, 32), 128 + 2 * HALF_SPAN)
    whiten(0, far, valid)
    pl.when(z < 4)(relay)
    pl.semaphore_wait(here, 15)
    send_planes(0, (FAR,))

    def rest(h, valid):
        def wide_block(b, carry):
            if h == 0:
                t_copy(b).wait()
            at = pl.multiple_of(EDGE + b * 256, EDGE)
            block(tv.at[:, pl.ds(at, 256)], at, 256)
            return carry

        lax.fori_loop(0, 4, wide_block, 0)

        def whiten_one(b, carry):
            if h == 0:
                pl.when(b != far)(lambda: whiten(h, b, valid))
            else:
                whiten(h, b, valid)
            return carry

        lax.fori_loop(0, 8, whiten_one, 0)

    rest(0, valid)
    send_planes(0, (3, 5, 1, 7, 2, 6, 0))
    fold(1)
    rest(1, valid_row(1))
    for pair in PHASES:
        send_planes(1, [off if off == 0 else lax.rem(8 + sign * off, 8) for off in pair])

    r, p = iota((128, 128), 1), iota((128, 128), 0)
    row_perm = (p == (r % 4) * 32 + (r // 4 % 2) * 16 + r // 8).astype(BF)
    for i in range(8):
        pick[i] = (iota((128, 512), 0) + i * 128 == small_ref[16:17, :]).astype(BF).T

    group = iota((128, 128), 1) // 16

    def swap(tiles):
        for bit in (4, 2, 1):
            high = group // bit % 2 == 1
            for i in range(8):
                if not i & bit:
                    a, b = tiles[i], tiles[i | bit]
                    tiles[i] = jnp.where(high, pltpu.roll(b, 16 * bit, 1), a)
                    tiles[i | bit] = jnp.where(high, b, pltpu.roll(a, 128 - 16 * bit, 1))
        return tiles

    for offs in ARRIVAL:
        places = [lax.rem(z + 8 - off, 8) for off in offs]
        mats = []
        for off, zs in zip(offs, places):
            part = pl.ds(zs * PLANE, PLANE)
            for h in range(CHUNKS):
                pltpu.make_async_copy(sendbuf.at[h, pl.ds(0, PLANE)], recv.at[h, part], recv_sem.at[h, off]).wait()
            got = recv[:, part].reshape(CHUNKS, 8, 4, 16, 128)
            wide = jnp.concatenate([got[:, i].reshape(128, 128) for i in range(8)], axis=1)
            ordered = jnp.dot(row_perm, wide, preferred_element_type=F32)
            tiles = [t.astype(BF) for t in swap([ordered[:, i * 128:i * 128 + 128] for i in range(8)])]
            bins = []
            for f in range(BINS):
                at = [(f * 2 + ri) * 16 for ri in range(2)]
                bins.append(jnp.concatenate([t[r:r + 16] for r in at for t in tiles], axis=0))
                d_ref[f, zs] = bins[f]
            mats.append(bins)
        picks = jnp.concatenate([pick[zs] for zs in places], axis=1)
        for f in range(BINS):
            mat = jnp.concatenate([bins[f] for bins in mats], axis=1)
            chosen = lax.dot_general(picks, mat, (((1,), (1,)), ((), ())), preferred_element_type=F32).astype(BF)
            s_ref[f] = chosen if offs == ARRIVAL[0] else s_ref[f] + chosen
    for h in range(CHUNKS):
        pltpu.make_async_copy(sendbuf.at[h, pl.ds(0, DEVS - 1)], recv.at[h, pl.ds(0, DEVS - 1)], send_sem.at[h]).wait()


def cross_kernel(d_ref, s_ref, o_hbm, buf, o_sem):
    outs = []
    for f in range(BINS):
        cc = jnp.concatenate([d_ref[f, i] for i in range(8)], axis=1)
        for ri in range(2):
            if ri == 1:
                cc = jnp.concatenate([cc[128:], -cc[:128]], axis=0)
            for m in range(0, 512, 256):
                part = pl.ds(m, 256)
                buf[ri, f, part] = jnp.dot(s_ref[f, part, :], cc, preferred_element_type=F32).astype(BF)
                out = pltpu.make_async_copy(buf.at[ri, f, part], o_hbm.at[ri, f, part], o_sem.at[ri, f, m // 256])
                out.start()
                outs.append(out)
    for out in outs:
        out.wait()


def body(table, traces, valid, sources):
    rows = traces.reshape(ROWS, NT)
    small = jnp.pad(valid.T, ((0, 8), (0, 480))) + jnp.pad(sources.reshape(1, 512), ((16, 7), (0, 0)))
    any_spec = pl.BlockSpec(memory_space=pl.ANY)
    vmem = pl.BlockSpec(memory_space=pltpu.VMEM)
    hbm = pl.BlockSpec(memory_space=pltpu.HBM)
    d, s = pl.pallas_call(
        front_kernel,
        out_shape=(jax.ShapeDtypeStruct((BINS, 8, 256, 128), BF), jax.ShapeDtypeStruct((BINS, 512, 256), BF)),
        in_specs=[hbm, hbm, vmem],
        out_specs=(vmem, vmem),
        scratch_shapes=[
            pltpu.VMEM((ROWS, NT), BF),
            pltpu.VMEM((2, F + 2 * EDGE, HALF), BF),
            pltpu.VMEM((2, 128 + 2 * HALF_SPAN, HALF), BF),
            pltpu.VMEM((NTP, ROWS), BF),
            pltpu.VMEM((HALF, 2 * LANES), BF),
            pltpu.VMEM((HALF, 2 * LANES), BF),
            pltpu.VMEM((2, F + 2 * EDGE, LANES), F32),
            pltpu.VMEM((F + 2 * EDGE, LANES), BF),
            pltpu.VMEM((F, LANES), F32),
            pltpu.VMEM((CHUNKS, DEVS, 16, 128), BF),
            pltpu.VMEM((CHUNKS, DEVS, 16, 128), BF),
            pltpu.VMEM((8, 512, 128), BF),
            pltpu.SemaphoreType.DMA((CHUNKS,)),
            pltpu.SemaphoreType.DMA((5,)),
            pltpu.SemaphoreType.DMA((CHUNKS,)),
            pltpu.SemaphoreType.DMA((CHUNKS, 8)),
            pltpu.SemaphoreType.REGULAR,
        ],
        compiler_params=pltpu.CompilerParams(collective_id=0, has_side_effects=True, vmem_limit_bytes=48 * 2**20),
    )(rows, table, small)
    return pl.pallas_call(
        cross_kernel,
        out_shape=jax.ShapeDtypeStruct((2, BINS, 512, 1024), BF),
        in_specs=[vmem, vmem],
        out_specs=any_spec,
        scratch_shapes=[
            pltpu.VMEM((2, BINS, 512, 1024), BF),
            pltpu.SemaphoreType.DMA((2, BINS, 2)),
        ],
        compiler_params=pltpu.CompilerParams(vmem_limit_bytes=24 * 2**20),
    )(d, s)


def solution(mesh):
    table = tables()

    def whole(traces, valid, sources):
        placed = (P(), P("tm", "chan", None), P("tm", "chan"), P())
        return jax.shard_map(
            body,
            mesh=mesh,
            in_specs=placed,
            out_specs=P(None, ("chan", "tm"), None, None),
            check_vma=False,
        )(jnp.asarray(table), traces, valid, sources)

    return whole
```

```python
import functools
import math

import jax
import jax.numpy as jnp
import numpy as np
from jax import lax
from jax.experimental import pallas as pl
from jax.experimental.pallas import tpu as pltpu
from jax.sharding import PartitionSpec as P

MESH = pl.DeviceIdType.MESH
F = 1024
LOW_BIN = 6
HALF_SPAN = 32
NT = 3000
NTP = 3072
HALF = NTP // 2
EDGE = 64
FAR = 4
DEVS = 256
PLANE = 32
BINS = 4
ROWS = 512
LANES = 256
CHUNKS = ROWS // LANES
PHASES = ((4, 1), (3, 7), (5, 0), (2, 6))
ARRIVAL = ((4,), (1, 7), (3, 5), (0,), (2, 6))
BF, F32 = jnp.bfloat16, jnp.float32


def tables():
    t = np.arange(HALF, dtype=np.int64)
    k = LOW_BIN + np.arange(F, dtype=np.int64)
    angle = 2.0 * math.pi / NT * ((k[:, None] * t[None, :]) % NT)
    taper = 0.5 - 0.5 * np.cos(2.0 * math.pi / NT * t)
    weight = np.where(t < NT // 2, 1.0, np.where(t == NT // 2, 0.5, 0.0)) * taper
    both = np.stack([weight * np.cos(angle), -weight * np.sin(angle)]).astype(np.float32)
    return np.pad(both, ((0, 0), (EDGE, EDGE), (0, 0))).astype(BF)


def me_at():
    ch, t = lax.axis_index("chan"), lax.axis_index("tm")
    z, y_hi = lax.div(ch, 8), lax.div(t, 2)
    x = lax.div(ch - z * 8, 2)
    return z, x, y_hi * 2 + ch - z * 8 - x * 2, t - y_hi * 2


def iota(shape, dim):
    return lax.broadcasted_iota(jnp.int32, shape, dim)


def front_kernel(x_hbm, t_hbm, valid_hbm, src_hbm, d_ref, s_ref, xv, tv, tv_first, xt, plus, minus, spec, amp, inv, sendbuf, recv, pick, early, valid_ref, src_ref, x_sem, t_sem, send_sem, recv_sem, small_sem, here):
    z, x, y, c = me_at()
    ch, t = lax.axis_index("chan"), lax.axis_index("tm")
    mine = ch * 4 + t
    sign = 1 - 2 * c
    far = lax.rem(z + FAR, 8)

    x_copies = [pltpu.make_async_copy(x_hbm.at[pl.ds(h * LANES, LANES)], xv.at[pl.ds(h * LANES, LANES)], x_sem.at[h]) for h in range(CHUNKS)]
    first_rows = pl.ds(pl.multiple_of(far * 128 + EDGE - HALF_SPAN, 32), 128 + 2 * HALF_SPAN)
    first_copy = pltpu.make_async_copy(t_hbm.at[:, first_rows], tv_first, t_sem.at[4])

    def t_copy(b):
        rows = pl.ds(EDGE + b * 256, 256)
        return pltpu.make_async_copy(t_hbm.at[:, rows], tv.at[:, rows], t_sem.at[b])

    x_copies[0].start()
    first_copy.start()
    small_copies = [pltpu.make_async_copy(valid_hbm, valid_ref, small_sem.at[0]), pltpu.make_async_copy(src_hbm, src_ref, small_sem.at[1])]
    for copy in small_copies:
        copy.start()

    ys = [lax.rem(y + j, 4) for j in range(4)]
    spots = [(lax.rem(ys[j], 2), lax.div(ys[j], 2) * 2 + c) for j in range(4)]
    column = [(lax.rem(ch + 8 * i, 64), t if j == 0 else t + 1 - 2 * c) for i in range(8) for j in range(2) if i or j]
    plane = [(z * 8 + lax.rem(x + i, 4) * 2 + spots[j][0], spots[j][1]) for i in range(4) for j in range(4) if i or j]

    def greet(devices, sem):
        for chan, tm in devices:
            pl.semaphore_signal(sem, inc=1, device_id={"chan": chan, "tm": tm}, device_id_type=MESH)

    barrier = pltpu.get_barrier_semaphore()
    greet(column + plane, barrier)

    spread = (iota((16, LANES), 1) % 16 == iota((16, LANES), 0)).astype(F32)
    low = iota((1, 8, LANES), 1) < 4
    band = (jnp.abs(iota((128, 256), 0) + 64 - iota((128, 256), 1)) <= HALF_SPAN).astype(BF)
    back = (iota((128, 256), 0) + iota((128, 256), 1) == NT - 22 * 128).astype(BF)
    k = iota((F, LANES), 0)
    inv[...] = 1.0 / (jnp.minimum(k + HALF_SPAN, F - 1) - jnp.maximum(k - HALF_SPAN, 0) + 1).astype(F32)
    amp[:EDGE, :] = jnp.zeros((EDGE, LANES), BF)
    amp[EDGE + F:, :] = jnp.zeros((EDGE, LANES), BF)
    xt[NTP - 128:, :] = jnp.zeros((128, ROWS), BF)

    def fold(h):
        lanes = slice(h * LANES, (h + 1) * LANES)
        x_copies[h].wait()
        for j in range(NT // 128):
            cols = slice(j * 128, (j + 1) * 128)
            xt[cols, lanes] = xv[lanes, cols].T
        tail = NT // 128 * 128
        xt[tail:NT, lanes] = xv[lanes, tail:NT].T
        for m in range(HALF // 128):
            at, there = slice(m * 128, m * 128 + 128), (22 - m) * 128
            ahead = xt[at, lanes].astype(F32)
            behind = jnp.dot(back, xt[there:there + 256, lanes], preferred_element_type=F32)
            for total, out in ((ahead + behind, plus), (ahead - behind, minus)):
                rounded = total.astype(BF)
                out[at, :LANES] = rounded
                out[at, LANES:] = (total - rounded.astype(F32)).astype(BF)

    def block(table, first, n):
        rows = pl.ds(first, n)
        re = jnp.dot(table[0], plus[...], preferred_element_type=F32)
        im = jnp.dot(table[1], minus[...], preferred_element_type=F32)
        re = re[:, :LANES] + re[:, LANES:]
        im = im[:, :LANES] + im[:, LANES:]
        spec[0, rows, :] = re
        spec[1, rows, :] = im
        power = re * re + im * im
        amp[rows, :] = (power * lax.rsqrt(jnp.maximum(power, 1e-37))).astype(BF)

    def valid_row(h):
        by_channel = lax.dot_general(valid_ref[...].astype(F32), spread, (((0,), (0,)), ((), ())), preferred_element_type=F32)
        mask = iota((32, LANES), 0) == h * (LANES // 16) + iota((32, LANES), 1) // 16
        return jnp.sum(jnp.where(mask, by_channel, 0.0), axis=0, keepdims=True)

    def whiten(h, b, valid):
        at = pl.multiple_of(b * 128, 128)
        rows = pl.ds(pl.multiple_of(EDGE + at, EDGE), 128)
        total = jnp.dot(band, amp[pl.ds(at, 256), :], preferred_element_type=F32)
        scale = valid / (total * inv[pl.ds(at, 128), :] + 1e-6)
        wr = (spec[0, rows, :] * scale).reshape(16, 8, LANES)
        wi = (spec[1, rows, :] * scale).reshape(16, 8, LANES)
        wa = jnp.where(low, wr, pltpu.roll(wi, 4, 1))
        wb = jnp.where(low, pltpu.roll(wr, 4, 1), wi)
        w = jnp.stack([wa, wb], axis=1)
        w = jnp.concatenate([w[..., :128], w[..., 128:]], axis=2)
        sendbuf[h, pl.ds(b * 32, 32)] = w.reshape(32, 16, 128).astype(BF)

    def send(h, n, off):
        xn, yn = lax.rem(x + lax.div(n, 8), 4), lax.rem(y + lax.rem(lax.div(n, 2), 4), 4)
        chan = lax.rem(z + off, 8) * 8 + xn * 2 + lax.rem(yn, 2)
        tm = lax.div(yn, 2) * 2 + lax.rem(c + n, 2)
        pltpu.make_async_remote_copy(
            src_ref=sendbuf.at[h, chan * 4 + tm], dst_ref=recv.at[h, mine], send_sem=send_sem.at[h],
            recv_sem=recv_sem.at[h, off], device_id={"chan": chan, "tm": tm}, device_id_type=MESH).start()

    def send_planes(h, offs):
        def one(n, carry):
            for off in offs:
                if isinstance(off, int) and off == 0:
                    pl.when(n > 0)(functools.partial(send, h, n, 0))
                else:
                    send(h, n, off)
            return carry

        lax.fori_loop(0, PLANE, one, 0)
        if any(isinstance(off, int) and off == 0 for off in offs):
            pltpu.make_async_copy(sendbuf.at[h, mine], recv.at[h, mine], recv_sem.at[h, 0]).start()

    def relay():
        pl.semaphore_wait(barrier, 30)
        greet(plane, here)

    pl.when(z >= 4)(relay)
    fold(0)
    for b in range(4):
        t_copy(b).start()
    x_copies[1].start()
    small_copies[0].wait()
    valid = valid_row(0)
    first_copy.wait()
    block(tv_first, pl.multiple_of(far * 128 + EDGE - HALF_SPAN, 32), 128 + 2 * HALF_SPAN)
    whiten(0, far, valid)
    pl.when(z < 4)(relay)
    pl.semaphore_wait(here, 15)
    send_planes(0, (FAR,))

    def rest(h, valid):
        def wide_block(b, carry):
            if h == 0:
                t_copy(b).wait()
            at = pl.multiple_of(EDGE + b * 256, EDGE)
            block(tv.at[:, pl.ds(at, 256)], at, 256)
            return carry

        lax.fori_loop(0, 4, wide_block, 0)

        def whiten_one(b, carry):
            if h == 0:
                pl.when(b != far)(lambda: whiten(h, b, valid))
            else:
                whiten(h, b, valid)
            return carry

        lax.fori_loop(0, 8, whiten_one, 0)

    rest(0, valid)
    send_planes(0, (3, 5, 1, 7, 2, 6, 0))
    fold(1)
    rest(1, valid_row(1))
    for pair in PHASES:
        send_planes(1, [off if off == 0 else lax.rem(8 + sign * off, 8) for off in pair])

    r, p = iota((64, 64), 1), iota((64, 64), 0)
    row_perm = (p == (r % 4) * 16 + (r // 4 % 2) * 8 + r // 8).astype(BF)
    small_copies[1].wait()
    for i in range(8):
        pick[i] = (iota((128, 512), 0) + i * 128 == src_ref[...]).astype(BF).T

    group = iota((64, 128), 1) // 16

    def swap(tiles):
        for bit in (4, 2, 1):
            high = group // bit % 2 == 1
            for i in range(8):
                if not i & bit:
                    a, b = tiles[i], tiles[i | bit]
                    tiles[i] = jnp.where(high, pltpu.roll(b, 16 * bit, 1), a)
                    tiles[i | bit] = jnp.where(high, b, pltpu.roll(a, 128 - 16 * bit, 1))
        return tiles

    def ordered(h, off):
        part = pl.ds(lax.rem(z + 8 - off, 8) * PLANE, PLANE)
        pltpu.make_async_copy(sendbuf.at[h, pl.ds(0, PLANE)], recv.at[h, part], recv_sem.at[h, off]).wait()
        got = recv[h, part].reshape(8, 4, 16, 128)
        wide = jnp.concatenate([got[i].reshape(64, 128) for i in range(8)], axis=1)
        rows = jnp.dot(row_perm, wide, preferred_element_type=F32)
        return swap([rows[:, i * 128:i * 128 + 128] for i in range(8)])

    for j, off in enumerate(ARRIVAL[-1]):
        for i, tile in enumerate(ordered(0, off)):
            early[j, i] = tile

    for offs in ARRIVAL:
        places = [lax.rem(z + 8 - off, 8) for off in offs]
        mats = []
        for j, (off, zs) in enumerate(zip(offs, places)):
            first = [early[j, i] for i in range(8)] if offs == ARRIVAL[-1] else ordered(0, off)
            second = ordered(1, off)
            bins = []
            for f in range(BINS):
                at = [(f * 2 + ri) * 8 for ri in range(2)]
                bins.append(jnp.concatenate([t[i][r:r + 8] for r in at for i in range(8) for t in (first, second)], axis=0).astype(BF))
                d_ref[f, zs] = bins[f]
            mats.append(bins)
        picks = jnp.concatenate([pick[zs] for zs in places], axis=1)
        for f in range(BINS):
            mat = jnp.concatenate([bins[f] for bins in mats], axis=1)
            chosen = lax.dot_general(picks, mat, (((1,), (1,)), ((), ())), preferred_element_type=F32).astype(BF)
            s_ref[f] = chosen if offs == ARRIVAL[0] else s_ref[f] + chosen
    for h in range(CHUNKS):
        pltpu.make_async_copy(sendbuf.at[h, pl.ds(0, DEVS - 1)], recv.at[h, pl.ds(0, DEVS - 1)], send_sem.at[h]).wait()


def cross_kernel(d_ref, s_ref, o_hbm, buf, o_sem):
    outs = []
    for f in range(BINS):
        cc = jnp.concatenate([d_ref[f, i] for i in range(8)], axis=1)
        for ri in range(2):
            if ri == 1:
                cc = jnp.concatenate([cc[128:], -cc[:128]], axis=0)
            for m in range(0, 512, 256):
                part = pl.ds(m, 256)
                buf[ri, f, part] = jnp.dot(s_ref[f, part, :], cc, preferred_element_type=F32).astype(BF)
                out = pltpu.make_async_copy(buf.at[ri, f, part], o_hbm.at[ri, f, part], o_sem.at[ri, f, m // 256])
                out.start()
                outs.append(out)
    for out in outs:
        out.wait()


def body(table, traces, valid, sources):
    rows = traces.reshape(ROWS, NT)
    any_spec = pl.BlockSpec(memory_space=pl.ANY)
    vmem = pl.BlockSpec(memory_space=pltpu.VMEM)
    hbm = pl.BlockSpec(memory_space=pltpu.HBM)
    d, s = pl.pallas_call(
        front_kernel,
        out_shape=(pltpu.VMEM((BINS, 8, 256, 128), BF), pltpu.VMEM((BINS, 512, 256), BF)),
        in_specs=[hbm, hbm, hbm, hbm],
        out_specs=(vmem, vmem),
        scratch_shapes=[
            pltpu.VMEM((ROWS, NT), BF),
            pltpu.VMEM((2, F + 2 * EDGE, HALF), BF),
            pltpu.VMEM((2, 128 + 2 * HALF_SPAN, HALF), BF),
            pltpu.VMEM((NTP, ROWS), BF),
            pltpu.VMEM((HALF, 2 * LANES), BF),
            pltpu.VMEM((HALF, 2 * LANES), BF),
            pltpu.VMEM((2, F + 2 * EDGE, LANES), F32),
            pltpu.VMEM((F + 2 * EDGE, LANES), BF),
            pltpu.VMEM((F, LANES), F32),
            pltpu.VMEM((CHUNKS, DEVS, 16, 128), BF),
            pltpu.VMEM((CHUNKS, DEVS, 16, 128), BF),
            pltpu.VMEM((8, 512, 128), BF),
            pltpu.VMEM((2, 8, 64, 128), F32),
            pltpu.VMEM((16, 32), jnp.int32),
            pltpu.VMEM((1, 512), jnp.int32),
            pltpu.SemaphoreType.DMA((CHUNKS,)),
            pltpu.SemaphoreType.DMA((5,)),
            pltpu.SemaphoreType.DMA((CHUNKS,)),
            pltpu.SemaphoreType.DMA((CHUNKS, 8)),
            pltpu.SemaphoreType.DMA((2,)),
            pltpu.SemaphoreType.REGULAR,
        ],
        compiler_params=pltpu.CompilerParams(collective_id=0, has_side_effects=True, vmem_limit_bytes=52 * 2**20),
    )(rows, table, valid.T, sources.reshape(1, 512))
    return pl.pallas_call(
        cross_kernel,
        out_shape=jax.ShapeDtypeStruct((2, BINS, 512, 1024), BF),
        in_specs=[vmem, vmem],
        out_specs=any_spec,
        scratch_shapes=[
            pltpu.VMEM((2, BINS, 512, 1024), BF),
            pltpu.SemaphoreType.DMA((2, BINS, 2)),
        ],
        compiler_params=pltpu.CompilerParams(vmem_limit_bytes=24 * 2**20),
    )(d, s)


def solution(mesh):
    table = tables()

    def whole(traces, valid, sources):
        placed = (P(), P("tm", "chan", None), P("tm", "chan"), P())
        return jax.shard_map(
            body,
            mesh=mesh,
            in_specs=placed,
            out_specs=P(None, ("chan", "tm"), None, None),
            check_vma=False,
        )(jnp.asarray(table), traces, valid, sources)

    return whole
```

```python
import functools
import math

import jax
import jax.numpy as jnp
import numpy as np
from jax import lax
from jax.experimental import pallas as pl
from jax.experimental.pallas import tpu as pltpu
from jax.sharding import PartitionSpec as P

MESH = pl.DeviceIdType.MESH
F = 1024
LOW_BIN = 6
HALF_SPAN = 32
NT = 3000
NTP = 3072
HALF = NTP // 2
EDGE = 64
FAR = 4
DEVS = 256
PLANE = 32
BINS = 4
ROWS = 512
LANES = 256
CHUNKS = ROWS // LANES
PHASES = ((4, 1), (3, 7), (5, 0), (2, 6))
ARRIVAL = ((4,), (1, 7), (3, 5), (0,), (2, 6))
BF, F32 = jnp.bfloat16, jnp.float32


def tables():
    t = np.arange(HALF, dtype=np.int64)
    k = LOW_BIN + np.arange(F, dtype=np.int64)
    angle = 2.0 * math.pi / NT * ((k[:, None] * t[None, :]) % NT)
    taper = 0.5 - 0.5 * np.cos(2.0 * math.pi / NT * t)
    weight = np.where(t < NT // 2, 1.0, np.where(t == NT // 2, 0.5, 0.0)) * taper
    both = np.stack([weight * np.cos(angle), -weight * np.sin(angle)]).astype(np.float32)
    return np.pad(both, ((0, 0), (EDGE, EDGE), (0, 0))).astype(BF)


def me_at():
    ch, t = lax.axis_index("chan"), lax.axis_index("tm")
    z, y_hi = lax.div(ch, 8), lax.div(t, 2)
    x = lax.div(ch - z * 8, 2)
    return z, x, y_hi * 2 + ch - z * 8 - x * 2, t - y_hi * 2


def iota(shape, dim):
    return lax.broadcasted_iota(jnp.int32, shape, dim)


def front_kernel(x_hbm, t_hbm, valid_hbm, src_hbm, d_ref, s_ref, xv, tv, tv_first, xt, plus, minus, spec, amp, inv, sendbuf, recv, pick, early, valid_ref, src_ref, x_sem, t_sem, send_sem, recv_sem, small_sem, here):
    z, x, y, c = me_at()
    ch, t = lax.axis_index("chan"), lax.axis_index("tm")
    mine = ch * 4 + t
    sign = 1 - 2 * c
    far = lax.rem(z + FAR, 8)

    x_copies = [pltpu.make_async_copy(x_hbm.at[pl.ds(h * LANES, LANES)], xv.at[pl.ds(h * LANES, LANES)], x_sem.at[h]) for h in range(CHUNKS)]
    first_rows = pl.ds(pl.multiple_of(far * 128 + EDGE - HALF_SPAN, 32), 128 + 2 * HALF_SPAN)
    first_copy = pltpu.make_async_copy(t_hbm.at[:, first_rows], tv_first, t_sem.at[4])

    def t_copy(b):
        rows = pl.ds(EDGE + b * 256, 256)
        return pltpu.make_async_copy(t_hbm.at[:, rows], tv.at[:, rows], t_sem.at[b])

    x_copies[0].start()
    first_copy.start()
    small_copies = [pltpu.make_async_copy(valid_hbm, valid_ref, small_sem.at[0]), pltpu.make_async_copy(src_hbm, src_ref, small_sem.at[1])]
    for copy in small_copies:
        copy.start()

    ys = [lax.rem(y + j, 4) for j in range(4)]
    spots = [(lax.rem(ys[j], 2), lax.div(ys[j], 2) * 2 + c) for j in range(4)]
    column = [(lax.rem(ch + 8 * i, 64), t if j == 0 else t + 1 - 2 * c) for i in range(8) for j in range(2) if i or j]
    plane = [(z * 8 + lax.rem(x + i, 4) * 2 + spots[j][0], spots[j][1]) for i in range(4) for j in range(4) if i or j]

    def greet(devices, sem):
        for chan, tm in devices:
            pl.semaphore_signal(sem, inc=1, device_id={"chan": chan, "tm": tm}, device_id_type=MESH)

    barrier = pltpu.get_barrier_semaphore()
    greet(column + plane, barrier)

    spread = (iota((16, LANES), 1) % 16 == iota((16, LANES), 0)).astype(F32)
    low = iota((1, 8, LANES), 1) < 4
    band = (jnp.abs(iota((128, 256), 0) + 64 - iota((128, 256), 1)) <= HALF_SPAN).astype(BF)
    back = (iota((128, 256), 0) + iota((128, 256), 1) == NT - 22 * 128).astype(BF)
    k = iota((F, LANES), 0)
    inv[...] = 1.0 / (jnp.minimum(k + HALF_SPAN, F - 1) - jnp.maximum(k - HALF_SPAN, 0) + 1).astype(F32)
    amp[:EDGE, :] = jnp.zeros((EDGE, LANES), BF)
    amp[EDGE + F:, :] = jnp.zeros((EDGE, LANES), BF)
    xt[NTP - 128:, :] = jnp.zeros((128, ROWS), BF)

    def fold(h):
        lanes = slice(h * LANES, (h + 1) * LANES)
        x_copies[h].wait()
        for j in range(NT // 128):
            cols = slice(j * 128, (j + 1) * 128)
            xt[cols, lanes] = xv[lanes, cols].T
        tail = NT // 128 * 128
        xt[tail:NT, lanes] = xv[lanes, tail:NT].T
        for m in range(HALF // 128):
            at, there = slice(m * 128, m * 128 + 128), (22 - m) * 128
            ahead = xt[at, lanes].astype(F32)
            behind = jnp.dot(back, xt[there:there + 256, lanes], preferred_element_type=F32)
            for total, out in ((ahead + behind, plus), (ahead - behind, minus)):
                rounded = total.astype(BF)
                out[at, :LANES] = rounded
                out[at, LANES:] = (total - rounded.astype(F32)).astype(BF)

    def block(table, first, n):
        rows = pl.ds(first, n)
        re = jnp.dot(table[0], plus[...], preferred_element_type=F32)
        im = jnp.dot(table[1], minus[...], preferred_element_type=F32)
        re = re[:, :LANES] + re[:, LANES:]
        im = im[:, :LANES] + im[:, LANES:]
        spec[0, rows, :] = re
        spec[1, rows, :] = im
        power = re * re + im * im
        amp[rows, :] = (power * lax.rsqrt(jnp.maximum(power, 1e-37))).astype(BF)

    def valid_row(h):
        by_channel = lax.dot_general(valid_ref[...].astype(F32), spread, (((0,), (0,)), ((), ())), preferred_element_type=F32)
        mask = iota((32, LANES), 0) == h * (LANES // 16) + iota((32, LANES), 1) // 16
        return jnp.sum(jnp.where(mask, by_channel, 0.0), axis=0, keepdims=True)

    def whiten(h, b, valid):
        at = pl.multiple_of(b * 128, 128)
        rows = pl.ds(pl.multiple_of(EDGE + at, EDGE), 128)
        total = jnp.dot(band, amp[pl.ds(at, 256), :], preferred_element_type=F32)
        scale = valid / (total * inv[pl.ds(at, 128), :] + 1e-6)
        wr = (spec[0, rows, :] * scale).reshape(16, 8, LANES)
        wi = (spec[1, rows, :] * scale).reshape(16, 8, LANES)
        wa = jnp.where(low, wr, pltpu.roll(wi, 4, 1))
        wb = jnp.where(low, pltpu.roll(wr, 4, 1), wi)
        w = jnp.stack([wa, wb], axis=1)
        w = jnp.concatenate([w[..., :128], w[..., 128:]], axis=2)
        sendbuf[h, pl.ds(b * 32, 32)] = w.reshape(32, 16, 128).astype(BF)

    def send(h, n, off):
        xn, yn = lax.rem(x + lax.div(n, 8), 4), lax.rem(y + lax.rem(lax.div(n, 2), 4), 4)
        chan = lax.rem(z + off, 8) * 8 + xn * 2 + lax.rem(yn, 2)
        tm = lax.div(yn, 2) * 2 + lax.rem(c + n, 2)
        pltpu.make_async_remote_copy(
            src_ref=sendbuf.at[h, chan * 4 + tm], dst_ref=recv.at[h, mine], send_sem=send_sem.at[h],
            recv_sem=recv_sem.at[h, off], device_id={"chan": chan, "tm": tm}, device_id_type=MESH).start()

    def send_planes(h, offs):
        def one(n, carry):
            for off in offs:
                if isinstance(off, int) and off == 0:
                    pl.when(n > 0)(functools.partial(send, h, n, 0))
                else:
                    send(h, n, off)
            return carry

        lax.fori_loop(0, PLANE, one, 0)
        if any(isinstance(off, int) and off == 0 for off in offs):
            pltpu.make_async_copy(sendbuf.at[h, mine], recv.at[h, mine], recv_sem.at[h, 0]).start()

    def relay():
        pl.semaphore_wait(barrier, 30)
        greet(plane, here)

    relay()
    fold(0)
    for b in range(4):
        t_copy(b).start()
    x_copies[1].start()
    small_copies[0].wait()
    valid = valid_row(0)
    first_copy.wait()
    block(tv_first, pl.multiple_of(far * 128 + EDGE - HALF_SPAN, 32), 128 + 2 * HALF_SPAN)
    whiten(0, far, valid)
    pl.semaphore_wait(here, 15)
    send_planes(0, (FAR,))

    def rest(h, valid):
        def wide_block(b, carry):
            if h == 0:
                t_copy(b).wait()
            at = pl.multiple_of(EDGE + b * 256, EDGE)
            block(tv.at[:, pl.ds(at, 256)], at, 256)
            return carry

        lax.fori_loop(0, 4, wide_block, 0)

        def whiten_one(b, carry):
            if h == 0:
                pl.when(b != far)(lambda: whiten(h, b, valid))
            else:
                whiten(h, b, valid)
            return carry

        lax.fori_loop(0, 8, whiten_one, 0)

    rest(0, valid)
    send_planes(0, (3, 5, 1, 7, 2, 6, 0))
    fold(1)
    rest(1, valid_row(1))
    for pair in PHASES:
        send_planes(1, [off if off == 0 else lax.rem(8 + sign * off, 8) for off in pair])

    r, p = iota((64, 64), 1), iota((64, 64), 0)
    row_perm = (p == (r % 4) * 16 + (r // 4 % 2) * 8 + r // 8).astype(BF)
    small_copies[1].wait()
    for i in range(8):
        pick[i] = (iota((128, 512), 0) + i * 128 == src_ref[...]).astype(BF).T

    group = iota((64, 128), 1) // 16

    def swap(tiles):
        for bit in (4, 2, 1):
            high = group // bit % 2 == 1
            for i in range(8):
                if not i & bit:
                    a, b = tiles[i], tiles[i | bit]
                    tiles[i] = jnp.where(high, pltpu.roll(b, 16 * bit, 1), a)
                    tiles[i | bit] = jnp.where(high, b, pltpu.roll(a, 128 - 16 * bit, 1))
        return tiles

    def ordered(h, off):
        part = pl.ds(lax.rem(z + 8 - off, 8) * PLANE, PLANE)
        pltpu.make_async_copy(sendbuf.at[h, pl.ds(0, PLANE)], recv.at[h, part], recv_sem.at[h, off]).wait()
        got = recv[h, part].reshape(8, 4, 16, 128)
        wide = jnp.concatenate([got[i].reshape(64, 128) for i in range(8)], axis=1)
        rows = jnp.dot(row_perm, wide, preferred_element_type=F32)
        return swap([rows[:, i * 128:i * 128 + 128] for i in range(8)])

    for j, off in enumerate(ARRIVAL[-1]):
        for i, tile in enumerate(ordered(0, off)):
            early[j, i] = tile

    for offs in ARRIVAL:
        places = [lax.rem(z + 8 - off, 8) for off in offs]
        mats = []
        for j, (off, zs) in enumerate(zip(offs, places)):
            first = [early[j, i] for i in range(8)] if offs == ARRIVAL[-1] else ordered(0, off)
            second = ordered(1, off)
            bins = []
            for f in range(BINS):
                at = [(f * 2 + ri) * 8 for ri in range(2)]
                bins.append(jnp.concatenate([t[i][r:r + 8] for r in at for i in range(8) for t in (first, second)], axis=0).astype(BF))
                d_ref[f, zs] = bins[f]
            mats.append(bins)
        picks = jnp.concatenate([pick[zs] for zs in places], axis=1)
        for f in range(BINS):
            mat = jnp.concatenate([bins[f] for bins in mats], axis=1)
            chosen = lax.dot_general(picks, mat, (((1,), (1,)), ((), ())), preferred_element_type=F32).astype(BF)
            s_ref[f] = chosen if offs == ARRIVAL[0] else s_ref[f] + chosen
    for h in range(CHUNKS):
        pltpu.make_async_copy(sendbuf.at[h, pl.ds(0, DEVS - 1)], recv.at[h, pl.ds(0, DEVS - 1)], send_sem.at[h]).wait()


def cross_kernel(d_ref, s_ref, o_hbm, buf, o_sem):
    outs = []
    for f in range(BINS):
        cc = jnp.concatenate([d_ref[f, i] for i in range(8)], axis=1)
        for ri in range(2):
            if ri == 1:
                cc = jnp.concatenate([cc[128:], -cc[:128]], axis=0)
            for m in range(0, 512, 256):
                part = pl.ds(m, 256)
                buf[ri, f, part] = jnp.dot(s_ref[f, part, :], cc, preferred_element_type=F32).astype(BF)
                out = pltpu.make_async_copy(buf.at[ri, f, part], o_hbm.at[ri, f, part], o_sem.at[ri, f, m // 256])
                out.start()
                outs.append(out)
    for out in outs:
        out.wait()


def body(table, traces, valid, sources):
    rows = traces.reshape(ROWS, NT)
    any_spec = pl.BlockSpec(memory_space=pl.ANY)
    vmem = pl.BlockSpec(memory_space=pltpu.VMEM)
    hbm = pl.BlockSpec(memory_space=pltpu.HBM)
    d, s = pl.pallas_call(
        front_kernel,
        out_shape=(pltpu.VMEM((BINS, 8, 256, 128), BF), pltpu.VMEM((BINS, 512, 256), BF)),
        in_specs=[hbm, hbm, hbm, hbm],
        out_specs=(vmem, vmem),
        scratch_shapes=[
            pltpu.VMEM((ROWS, NT), BF),
            pltpu.VMEM((2, F + 2 * EDGE, HALF), BF),
            pltpu.VMEM((2, 128 + 2 * HALF_SPAN, HALF), BF),
            pltpu.VMEM((NTP, ROWS), BF),
            pltpu.VMEM((HALF, 2 * LANES), BF),
            pltpu.VMEM((HALF, 2 * LANES), BF),
            pltpu.VMEM((2, F + 2 * EDGE, LANES), F32),
            pltpu.VMEM((F + 2 * EDGE, LANES), BF),
            pltpu.VMEM((F, LANES), F32),
            pltpu.VMEM((CHUNKS, DEVS, 16, 128), BF),
            pltpu.VMEM((CHUNKS, DEVS, 16, 128), BF),
            pltpu.VMEM((8, 512, 128), BF),
            pltpu.VMEM((2, 8, 64, 128), F32),
            pltpu.VMEM((16, 32), jnp.int32),
            pltpu.VMEM((1, 512), jnp.int32),
            pltpu.SemaphoreType.DMA((CHUNKS,)),
            pltpu.SemaphoreType.DMA((5,)),
            pltpu.SemaphoreType.DMA((CHUNKS,)),
            pltpu.SemaphoreType.DMA((CHUNKS, 8)),
            pltpu.SemaphoreType.DMA((2,)),
            pltpu.SemaphoreType.REGULAR,
        ],
        compiler_params=pltpu.CompilerParams(collective_id=0, has_side_effects=True, vmem_limit_bytes=52 * 2**20),
    )(rows, table, valid.T, sources.reshape(1, 512))
    return pl.pallas_call(
        cross_kernel,
        out_shape=jax.ShapeDtypeStruct((2, BINS, 512, 1024), BF),
        in_specs=[vmem, vmem],
        out_specs=any_spec,
        scratch_shapes=[
            pltpu.VMEM((2, BINS, 512, 1024), BF),
            pltpu.SemaphoreType.DMA((2, BINS, 2)),
        ],
        compiler_params=pltpu.CompilerParams(vmem_limit_bytes=24 * 2**20),
    )(d, s)


def solution(mesh):
    table = tables()

    def whole(traces, valid, sources):
        placed = (P(), P("tm", "chan", None), P("tm", "chan"), P())
        return jax.shard_map(
            body,
            mesh=mesh,
            in_specs=placed,
            out_specs=P(None, ("chan", "tm"), None, None),
            check_vma=False,
        )(jnp.asarray(table), traces, valid, sources)

    return whole
```
